32 devices in a mesh: dp: 32 (over z, y, x, core).
Axes of the slice: x: 2, y: 2, z: 4, core: 2. Of those that a mesh axis runs over, the one named last changes fastest.
Arguments:
- spikes: bfloat16 [128, 64, 256], P('dp'), may hold values from -6 to 6
- block_lists: int32 [128, 2], P('dp'), may hold values from 0 to 511, as said below
- bin_counts: int32 [128], P('dp'), may hold values from 1 to 64, as said below
- readin_table: bfloat16 [512, 128, 1024], P('dp'), may hold values from -0.375 to 0.375
- norm_gain: float32 [1024], replicated, may hold values from 0.1 to 1.9
- w_in: bfloat16 [1024, 2048], replicated, may hold values from -0.1875 to 0.1875
- w_out: bfloat16 [2048, 1024], replicated, may hold values from -0.125 to 0.125
- cotangent: bfloat16 [128, 64, 1024], P(None, 'dp'), may hold values from -6 to 6
Outputs:
- encoded: bfloat16 [128, 64, 1024], P(None, 'dp')
- readin_grad: bfloat16 [512, 128, 1024], P('dp')
The draws below stay inside these ranges and needn't reach their ends.
Inputs may be any that keep to these rules, and one draw needn't show every extreme that they name: `block_lists`: block k is held by device k // 16. The sessions of device d are d * 4 to (d + 1) * 4 - 1; of their 8 entries exactly 1 name blocks held by each of the devices d, d + 1, ..., d + 7, counted modulo the number of devices. `bin_counts`: among the sessions of every device one has all 64 bins valid.
All inputs are finite; a program needn't handle non-finite values.
Results may differ from the reference program's by a relative error of at most 0.0056.
Values may be sent and summed in bfloat16 or wider, within the bound.
A program may use at most 128 MiB of HBM per device.

```python
import jax
import jax.numpy as jnp
from jax import lax

D = 1024
FF = 2048
UB = 128
NB = 2
SESS_DEV = 4
TAB_DEV = 16
CAP = 1
SESSIONS = 128
BINS = 64
BLOCKS = 512
N_DP = 32


def draw_block_lists(key, part):
    devices = SESSIONS // SESS_DEV
    slot_count = SESS_DEV * NB
    base_key = jax.random.fold_in(key, 11)
    first, second, third = jax.random.split(base_key, 3)
    pattern = jnp.arange(slot_count, dtype=jnp.int32) // CAP
    device_keys = jax.random.split(first, devices)
    offsets = jax.vmap(lambda one_key: jax.random.permutation(one_key, pattern))(device_keys)
    local_rows = jax.random.randint(second, (devices, slot_count), 0, TAB_DEV)
    chosen = jax.random.randint(third, (devices, 1), 0, slot_count)
    local_rows = jnp.where(jnp.arange(slot_count)[None, :] == chosen, TAB_DEV - 1, local_rows)
    owners = jnp.mod(jnp.arange(devices, dtype=jnp.int32)[:, None] + offsets, devices)
    return (owners * TAB_DEV + local_rows).reshape(SESSIONS, NB).astype(jnp.int32)


def draw_bin_counts(key, part):
    devices = SESSIONS // SESS_DEV
    base_key = jax.random.fold_in(key, 23)
    first, second = jax.random.split(base_key)
    counts = jax.random.randint(first, (devices, SESS_DEV), 1, BINS + 1)
    chosen = jax.random.randint(second, (devices, 1), 0, SESS_DEV)
    counts = jnp.where(jnp.arange(SESS_DEV)[None, :] == chosen, BINS, counts)
    return counts.reshape(SESSIONS).astype(jnp.int32)


def steps_of(own_key, shape, cuts, least, high):
    gain = 1.0
    for dim, blocks in cuts:
        steps = jax.random.uniform(jax.random.fold_in(jax.random.fold_in(own_key, 6), dim), (blocks,), jnp.float32, least / len(cuts), high / len(cuts))
        gain = gain * jnp.repeat(jnp.exp(steps), shape[dim] // blocks).reshape((-1,) + (1,) * (len(shape) - 1 - dim))
    return gain


def normal_values(key, extent, width, bound, shards=(), held_as=jnp.bfloat16):
    loudness = steps_of(key, extent, shards, -0.22, 0.18) if shards else 1.0
    array = jax.random.normal(key, extent, jnp.float32) * width * loudness
    return jnp.minimum(jnp.maximum(array, -bound), bound).astype(held_as)


def setup_inputs(seed: int = 0) -> dict:
    splits = jax.random.split(jax.random.key(seed), 9)
    spikes = normal_values(splits[0], (SESSIONS, BINS, NB * UB), 1.0, 6.0, ((0, 32),))
    block_lists = draw_block_lists(jax.random.fold_in(splits[8], 71), 0)
    bin_counts = draw_bin_counts(jax.random.fold_in(splits[8], 71), 0)
    readin_table = normal_values(splits[3], (BLOCKS, UB, D), (NB * UB) ** -0.5, 0.375, ((0, 32),))
    norm_gain = jnp.clip(1.0 + 0.18 * jax.random.normal(splits[4], (D,), jnp.float32), 0.1, 1.9)
    w_in = normal_values(splits[5], (D, FF), D ** -0.5, 0.1875)
    w_out = normal_values(splits[6], (FF, D), FF ** -0.5, 0.125)
    cotangent = normal_values(splits[7], (SESSIONS, BINS, D), 1.0, 6.0, ((1, 32),))
    return {"spikes": spikes, "block_lists": block_lists, "bin_counts": bin_counts, "readin_table": readin_table, "norm_gain": norm_gain, "w_in": w_in, "w_out": w_out, "cotangent": cotangent}


EPS = 1e-06

def gelu_tanh(values):
    return jax.nn.gelu(values, approximate=True)

def encode_rows(latent_rows, norm_gain, w_in, w_out, cot_rows):
    inputs = latent_rows.astype(jnp.float32)
    mean_square = lax.optimization_barrier(jnp.mean(inputs * inputs, axis=-1, keepdims=True))
    inverse_rms = lax.rsqrt(mean_square + EPS)
    normed = (inputs * inverse_rms * norm_gain).astype(jnp.bfloat16)
    hidden_pre = jnp.dot(normed, w_in, preferred_element_type=jnp.float32)
    activated, pullback = jax.vjp(gelu_tanh, hidden_pre)
    activated = activated.astype(jnp.bfloat16)
    encoded = (inputs + jnp.dot(activated, w_out, preferred_element_type=jnp.float32)).astype(jnp.bfloat16)
    grad_activated = lax.dot_general(cot_rows, w_out, (((1,), (1,)), ((), ())), preferred_element_type=jnp.float32)
    grad_hidden = pullback(grad_activated)[0].astype(jnp.bfloat16)
    grad_normed = lax.dot_general(grad_hidden, w_in, (((1,), (1,)), ((), ())), preferred_element_type=jnp.float32)
    scaled = grad_normed * norm_gain
    grad_inputs = inverse_rms * scaled - inputs * (inverse_rms * inverse_rms * inverse_rms) * lax.optimization_barrier(jnp.mean(scaled * inputs, axis=-1, keepdims=True))
    returned = (cot_rows.astype(jnp.float32) + grad_inputs).astype(jnp.bfloat16)
    return (encoded, returned)

def reference(spikes, block_lists, bin_counts, readin_table, norm_gain, w_in, w_out, cotangent):
    slot_count = SESS_DEV * NB
    spikes_dev = spikes.reshape(N_DP, SESS_DEV, BINS, NB, UB)
    lists_dev = block_lists.reshape(N_DP, slot_count).astype(jnp.int32)
    counts_dev = bin_counts.reshape(N_DP, SESS_DEV)
    cot_dev = cotangent.reshape(N_DP, SESS_DEV, BINS, D)

    def device_step(total, items):
        spikes_here, lists_here, counts_here, cot_here = items
        weights = jnp.take(readin_table, lists_here, axis=0).astype(jnp.float32).reshape(SESS_DEV, NB, UB, D)
        spikes_wide = spikes_here.astype(jnp.float32)
        latent = jnp.einsum('stnu,snud->std', spikes_wide, weights, precision=lax.Precision.HIGHEST)
        valid = (lax.broadcasted_iota(jnp.int32, (SESS_DEV, BINS), 1) < counts_here[:, None]).astype(jnp.float32)[:, :, None]
        latent = (latent * valid).astype(jnp.bfloat16)
        encoded, returned = encode_rows(latent.reshape(-1, D), norm_gain, w_in, w_out, cot_here.reshape(-1, D))
        grad_latent = (returned.reshape(SESS_DEV, BINS, D).astype(jnp.float32) * valid).astype(jnp.bfloat16)
        slot_grads = jnp.einsum('stnu,std->snud', spikes_wide, grad_latent.astype(jnp.float32), precision=lax.Precision.HIGHEST)
        total = total.at[lists_here].add(slot_grads.reshape(slot_count, UB, D))
        return (total, encoded.reshape(SESS_DEV, BINS, D))
    start = jnp.zeros((BLOCKS, UB, D), jnp.float32)
    total, encoded = lax.scan(device_step, start, (spikes_dev, lists_dev, counts_dev, cot_dev))
    return (encoded.reshape(SESSIONS, BINS, D), total.astype(jnp.bfloat16))
```

```python
import functools

import jax
import jax.numpy as jnp
from jax import lax
from jax.experimental import pallas as pl
from jax.experimental.pallas import tpu as pltpu
from jax.sharding import PartitionSpec as P

NEAR = 8
EPS = 1e-06
LANES = 128
TILE = 256
FF_TILE = 512
GELU_C = 0.7978845608028654
GELU_A = 0.044715
BF16 = jnp.bfloat16
F32 = jnp.float32


def remote(src, dst, send_sem, recv_sem, device):
    return pltpu.make_async_remote_copy(
        src_ref=src,
        dst_ref=dst,
        send_sem=send_sem,
        recv_sem=recv_sem,
        device_id=(device,),
        device_id_type=pl.DeviceIdType.MESH,
    )


def exchange_kernel(
    n,
    table_rows,
    lists_ref,
    counts_ref,
    spikes_ref,
    table_hbm,
    gain_ref,
    w_in_hbm,
    w_out_hbm,
    cot_ref,
    encoded_ref,
    marked_ref,
    rows_hbm,
    table,
    w_in,
    w_out,
    spike_send,
    spike_recv,
    part_send,
    part_recv,
    route,
    returned,
    grad_send,
    acc_enc,
    acc_grad,
    load_sems,
    spike_ss,
    spike_rs,
    part_ss,
    part_rs,
    grad_ss,
    grad_rs,
):
    me = lax.axis_index("dp")
    loads = [
        pltpu.make_async_copy(table_hbm, table, load_sems.at[0]),
        pltpu.make_async_copy(w_in_hbm, w_in, load_sems.at[1]),
        pltpu.make_async_copy(w_out_hbm, w_out, load_sems.at[2]),
    ]
    for load in loads:
        load.start()

    barrier = pltpu.get_barrier_semaphore()

    def greet(i, carry):
        pl.semaphore_signal(
            barrier,
            inc=1,
            device_id=(lax.rem(me + i, n),),
            device_id_type=pl.DeviceIdType.MESH,
        )
        return carry

    lax.fori_loop(1, n, greet, 0)

    sessions, bins, _ = spikes_ref.shape
    blocks = 2
    depth = bins // n
    chunk = NEAR * depth
    width = table.shape[1]
    rows = n * chunk
    encode_rows = encoded_ref.shape[0]

    weights = []
    locals_ = []
    for s in range(sessions):
        for b in range(blocks):
            entry = lists_ref[s * blocks + b]
            weights.append(lax.rem(entry // table_rows - me + n, n))
            locals_.append(lax.rem(entry, table_rows))
    valid = [
        lax.broadcasted_iota(jnp.int32, (bins, LANES), 0) < counts_ref[s] for s in range(sessions)
    ]
    slabs = []
    for s in range(sessions):
        for b in range(blocks):
            slab = spikes_ref[s, :, b * LANES : (b + 1) * LANES].astype(F32)
            slabs.append(jnp.where(valid[s], slab, 0.0))
    for o in range(NEAR):
        total = jnp.zeros((bins, LANES), F32)
        mark_row = jnp.int32(0)
        mark_session = jnp.int32(0)
        for i in range(sessions * blocks):
            hit = jnp.where(weights[i] == o, 1, 0)
            total = total + slabs[i] * hit.astype(F32)
            mark_row = mark_row + hit * locals_[i]
            mark_session = mark_session + hit * (i // blocks)
        target = spike_recv if o == 0 else spike_send
        target[o, :, 0:LANES] = total.astype(BF16)
        target[o, :, LANES : 2 * LANES] = jnp.full((bins, LANES), mark_row.astype(F32)).astype(BF16)
        target[o, :, 2 * LANES : 3 * LANES] = jnp.full(
            (bins, LANES), mark_session.astype(F32)
        ).astype(BF16)

    pl.semaphore_wait(barrier, n - 1)
    for o in range(1, NEAR):
        remote(
            spike_send.at[o], spike_recv.at[o], spike_ss.at[o], spike_rs.at[o], lax.rem(me + o, n)
        ).start()
    loads[0].wait()
    for o in range(1, NEAR):
        remote(
            spike_send.at[o], spike_recv.at[o], spike_ss.at[o], spike_rs.at[o], lax.rem(me + o, n)
        ).wait()

    def part_copy(j):
        i = lax.rem(j - me + n, n)
        return remote(
            part_send.at[pl.ds(pl.multiple_of(j * chunk, chunk), chunk), :],
            part_recv.at[pl.ds(pl.multiple_of(me * chunk, chunk), chunk), :],
            part_ss.at[i],
            part_rs.at[i],
            j,
        )

    def grad_copy(j):
        i = lax.rem(j - me + n, n)
        return remote(
            grad_send.at[pl.ds(pl.multiple_of(j * chunk, chunk), chunk), :],
            rows_hbm.at[pl.ds(pl.multiple_of(me * chunk, chunk), chunk), :],
            grad_ss.at[i],
            grad_rs.at[i],
            j,
        )

    per_tile = TILE // chunk

    def project(r, carry):
        start = pl.multiple_of(r * TILE, TILE)
        q = lax.broadcasted_iota(jnp.int32, (TILE, NEAR * bins), 0) + r * TILE
        c = lax.broadcasted_iota(jnp.int32, (TILE, NEAR * bins), 1)
        source = lax.rem(q, chunk) // depth * bins + q // chunk * depth + lax.rem(q, depth)
        order = jnp.where(source == c, 1.0, 0.0).astype(BF16)
        received = spike_recv[...].reshape(NEAR * bins, 3 * LANES)
        moved = jnp.dot(order, received, preferred_element_type=F32)
        values = moved[:, 0:LANES]
        holder = moved[:, LANES : 2 * LANES]
        marked_ref[pl.ds(start, TILE), :] = moved[:, 0 : 2 * LANES].astype(BF16)
        spread = jnp.concatenate(
            [jnp.where(holder == float(k), values, 0.0).astype(BF16) for k in range(table_rows)],
            axis=1,
        )
        part_send[pl.ds(start, TILE), 0:width] = jnp.dot(
            spread, table[...], preferred_element_type=F32
        ).astype(BF16)
        part_send[pl.ds(start, TILE), width : width + LANES] = moved[
            :, 2 * LANES : 3 * LANES
        ].astype(BF16)

        def send(x, inner):
            j = r * per_tile + x

            @pl.when(j != me)
            def _():
                part_copy(j).start()

            return inner

        lax.fori_loop(0, per_tile, send, 0)
        return carry

    lax.fori_loop(0, rows // TILE, project, 0)
    own = pl.ds(pl.multiple_of(me * chunk, chunk), chunk)
    part_recv[own, :] = part_send[own, :]

    def wait_part(i, carry):
        part_copy(lax.rem(me + i, n)).wait()
        return carry

    lax.fori_loop(1, n, wait_part, 0)

    def build(r, carry):
        start = pl.multiple_of(r * TILE, TILE)
        q = lax.broadcasted_iota(jnp.int32, (TILE, encode_rows), 0) + r * TILE
        c = lax.broadcasted_iota(jnp.int32, (TILE, encode_rows), 1)
        origin = lax.rem(q // chunk - lax.rem(q, chunk) // depth + n, n)
        base = c - origin * (sessions * depth) - lax.rem(q, depth)
        which = part_recv[pl.ds(start, TILE), width : width + LANES].astype(F32)[:, 0:1]
        route[pl.ds(start, TILE), :] = jnp.where(
            base.astype(F32) == which * float(depth), 1.0, 0.0
        ).astype(BF16)
        return carry

    lax.fori_loop(0, rows // TILE, build, 0)
    loads[1].wait()
    loads[2].wait()

    def encode(e, carry):
        start = pl.multiple_of(e * TILE, TILE)
        here = pl.ds(start, TILE)
        latent = lax.dot_general(
            route[:, here],
            part_recv[:, 0:width],
            (((0,), (0,)), ((), ())),
            preferred_element_type=F32,
        ).astype(BF16)
        inputs = latent.astype(F32)
        gain = gain_ref[...]
        inverse = lax.rsqrt(jnp.mean(inputs * inputs, axis=-1, keepdims=True) + EPS)
        normed = (inputs * inverse * gain).astype(BF16)
        cot = cot_ref[here, :]
        acc_enc[...] = inputs
        acc_grad[...] = jnp.zeros_like(acc_grad)

        def hidden(f, inner):
            cols = pl.ds(pl.multiple_of(f * FF_TILE, FF_TILE), FF_TILE)
            first = w_in[:, cols]
            second = w_out[cols, :]
            v = jnp.dot(normed, first, preferred_element_type=F32)
            v2 = v * v
            th = jnp.tanh(GELU_C * (v + GELU_A * v * v2))
            half = 0.5 * (1.0 + th)
            slope = half + 0.5 * v * (1.0 - th * th) * (GELU_C * (1.0 + 3.0 * GELU_A * v2))
            acc_enc[...] += jnp.dot((v * half).astype(BF16), second, preferred_element_type=F32)
            back = lax.dot_general(
                cot, second, (((1,), (1,)), ((), ())), preferred_element_type=F32
            )
            acc_grad[...] += lax.dot_general(
                (back * slope).astype(BF16),
                first,
                (((1,), (1,)), ((), ())),
                preferred_element_type=F32,
            )
            return inner

        lax.fori_loop(0, w_in.shape[1] // FF_TILE, hidden, 0)
        encoded_ref[here, :] = acc_enc[...].astype(BF16)
        scaled = acc_grad[...] * gain
        grad = inverse * scaled - inputs * (inverse * inverse * inverse) * jnp.mean(
            scaled * inputs, axis=-1, keepdims=True
        )
        returned[here, :] = (cot.astype(F32) + grad).astype(BF16)
        return carry

    lax.fori_loop(0, encode_rows // TILE, encode, 0)

    def give_back(r, carry):
        start = pl.multiple_of(r * TILE, TILE)
        grad_send[pl.ds(start, TILE), :] = jnp.dot(
            route[pl.ds(start, TILE), :], returned[...], preferred_element_type=F32
        ).astype(BF16)

        def send(x, inner):
            j = r * per_tile + x

            @pl.when(j != me)
            def _():
                grad_copy(j).start()

            return inner

        lax.fori_loop(0, per_tile, send, 0)
        return carry

    lax.fori_loop(0, rows // TILE, give_back, 0)
    keep = pltpu.make_async_copy(grad_send.at[own, :], rows_hbm.at[own, :], load_sems.at[3])
    keep.start()
    keep.wait()

    def wait_grad(i, carry):
        grad_copy(lax.rem(me + i, n)).wait()
        return carry

    lax.fori_loop(1, n, wait_grad, 0)


def grad_kernel(per_step, marked_ref, rows_ref, out_ref):
    first = pl.program_id(0) * per_step
    values = marked_ref[:, 0:LANES].astype(F32)
    holder = marked_ref[:, LANES : 2 * LANES].astype(F32)
    spread = jnp.concatenate(
        [
            jnp.where(holder == (first + k).astype(F32), values, 0.0).astype(BF16)
            for k in range(per_step)
        ],
        axis=1,
    )
    out_ref[...] = lax.dot_general(
        spread, rows_ref[...], (((0,), (0,)), ((), ())), preferred_element_type=F32
    ).astype(BF16)


def on_device(n, spikes, block_lists, bin_counts, readin_table, norm_gain, w_in, w_out, cotangent):
    sessions, bins, columns = spikes.shape
    table_rows, unit_block, width = readin_table.shape
    total_sessions, depth, _ = cotangent.shape
    hidden = w_in.shape[1]
    chunk = NEAR * depth
    rows = n * chunk
    encode_rows = total_sessions * depth
    vmem = pl.BlockSpec(memory_space=pltpu.VMEM)
    smem = pl.BlockSpec(memory_space=pltpu.SMEM)
    hbm = pl.BlockSpec(memory_space=pl.ANY)
    encoded, marked, grad_rows = pl.pallas_call(
        functools.partial(exchange_kernel, n, table_rows),
        out_shape=(
            jax.ShapeDtypeStruct((encode_rows, width), BF16),
            jax.ShapeDtypeStruct((rows, 2 * LANES), BF16),
            jax.ShapeDtypeStruct((rows, width), BF16),
        ),
        in_specs=[smem, smem, vmem, hbm, vmem, hbm, hbm, vmem],
        out_specs=(vmem, vmem, hbm),
        scratch_shapes=[
            pltpu.VMEM((table_rows * unit_block, width), BF16),
            pltpu.VMEM((width, hidden), BF16),
            pltpu.VMEM((hidden, width), BF16),
            pltpu.VMEM((NEAR, bins, 3 * LANES), BF16),
            pltpu.VMEM((NEAR, bins, 3 * LANES), BF16),
            pltpu.VMEM((rows, width + LANES), BF16),
            pltpu.VMEM((rows, width + LANES), BF16),
            pltpu.VMEM((rows, encode_rows), BF16),
            pltpu.VMEM((encode_rows, width), BF16),
            pltpu.VMEM((rows, width), BF16),
            pltpu.VMEM((TILE, width), F32),
            pltpu.VMEM((TILE, width), F32),
            pltpu.SemaphoreType.DMA((4,)),
            pltpu.SemaphoreType.DMA((NEAR,)),
            pltpu.SemaphoreType.DMA((NEAR,)),
            pltpu.SemaphoreType.DMA((n,)),
            pltpu.SemaphoreType.DMA((n,)),
            pltpu.SemaphoreType.DMA((n,)),
            pltpu.SemaphoreType.DMA((n,)),
        ],
        compiler_params=pltpu.CompilerParams(
            collective_id=0, has_side_effects=True, vmem_limit_bytes=58 * 1024 * 1024
        ),
    )(
        block_lists.reshape(-1),
        bin_counts,
        spikes,
        readin_table.reshape(table_rows * unit_block, width),
        norm_gain.reshape(1, width),
        w_in,
        w_out,
        cotangent.reshape(encode_rows, width),
    )
    per_step = 2
    total = pl.pallas_call(
        functools.partial(grad_kernel, per_step),
        grid=(table_rows // per_step,),
        out_shape=jax.ShapeDtypeStruct((table_rows * unit_block, width), BF16),
        in_specs=[
            pl.BlockSpec((rows, 2 * LANES), lambda i: (0, 0)),
            pl.BlockSpec((rows, width), lambda i: (0, 0)),
        ],
        out_specs=pl.BlockSpec((per_step * unit_block, width), lambda i: (i, 0)),
        compiler_params=pltpu.CompilerParams(vmem_limit_bytes=40 * 1024 * 1024),
    )(marked, grad_rows)
    return (
        encoded.reshape(total_sessions, depth, width),
        total.reshape(table_rows, unit_block, width),
    )


def solution(mesh):
    n = mesh.shape["dp"]
    return jax.shard_map(
        functools.partial(on_device, n),
        mesh=mesh,
        in_specs=(
            P("dp", None, None),
            P("dp", None),
            P("dp"),
            P("dp", None, None),
            P(),
            P(),
            P(),
            P(None, "dp", None),
        ),
        out_specs=(P(None, "dp", None), P("dp", None, None)),
        check_vma=False,
    )
```

```python
import functools

import jax
import jax.numpy as jnp
from jax import lax
from jax.experimental import pallas as pl
from jax.experimental.pallas import tpu as pltpu
from jax.sharding import PartitionSpec as P

NEAR = 8
EPS = 1e-06
LANES = 128
TILE = 256
FF_TILE = 512
GELU_C = 0.7978845608028654
GELU_A = 0.044715
BF16 = jnp.bfloat16
F32 = jnp.float32


def remote(src, dst, send_sem, recv_sem, device):
    return pltpu.make_async_remote_copy(
        src_ref=src,
        dst_ref=dst,
        send_sem=send_sem,
        recv_sem=recv_sem,
        device_id=(device,),
        device_id_type=pl.DeviceIdType.MESH,
    )


def exchange_kernel(
    n,
    table_rows,
    lists_ref,
    counts_ref,
    spikes_ref,
    table_hbm,
    gain_ref,
    w_in_hbm,
    w_out_hbm,
    cot_hbm,
    encoded_hbm,
    marked_ref,
    rows_hbm,
    table,
    w_in,
    w_out,
    spike_send,
    spike_recv,
    part_send,
    part_recv,
    cot_recv,
    enc_send,
    route,
    returned,
    grad_send,
    slopes,
    accumulator,
    load_sems,
    spike_ss,
    spike_rs,
    part_ss,
    part_rs,
    grad_ss,
    grad_rs,
    cot_ss,
    cot_rs,
    enc_ss,
    enc_rs,
):
    me = lax.axis_index("dp")
    sessions, bins, _ = spikes_ref.shape
    blocks = 2
    depth = bins // n
    chunk = sessions * depth
    width = table.shape[1]
    rows = NEAR * bins
    encode_rows = returned.shape[0]
    mine = pl.ds(me * sessions, sessions)
    loads = [
        pltpu.make_async_copy(table_hbm, table, load_sems.at[0]),
        pltpu.make_async_copy(w_in_hbm, w_in, load_sems.at[1]),
        pltpu.make_async_copy(w_out_hbm, w_out, load_sems.at[2]),
        pltpu.make_async_copy(cot_hbm.at[mine], cot_recv.at[me], load_sems.at[3]),
    ]
    for load in loads:
        load.start()

    barrier = pltpu.get_barrier_semaphore()

    def greet(i, carry):
        pl.semaphore_signal(
            barrier,
            inc=1,
            device_id=(lax.rem(me + i, n),),
            device_id_type=pl.DeviceIdType.MESH,
        )
        return carry

    lax.fori_loop(1, n, greet, 0)

    offsets = []
    locals_ = []
    for i in range(sessions * blocks):
        entry = lists_ref[i // blocks, i % blocks]
        offsets.append(lax.rem(entry // table_rows - me + n, n))
        locals_.append(lax.rem(entry, table_rows))
    valid = [
        lax.broadcasted_iota(jnp.int32, (bins, LANES), 0) < counts_ref[s] for s in range(sessions)
    ]
    slabs = []
    for s in range(sessions):
        for b in range(blocks):
            slab = spikes_ref[s, :, b * LANES : (b + 1) * LANES].astype(F32)
            slabs.append(jnp.where(valid[s], slab, 0.0))
    owners = []
    for o in range(NEAR):
        total = jnp.zeros((bins, LANES), F32)
        mark_row = jnp.int32(0)
        mark_session = jnp.int32(0)
        for i in range(sessions * blocks):
            hit = jnp.where(offsets[i] == o, 1, 0)
            total = total + slabs[i] * hit.astype(F32)
            mark_row = mark_row + hit * locals_[i]
            mark_session = mark_session + hit * (i // blocks)
        owners.append(mark_session)
        target = spike_recv if o == 0 else spike_send
        target[o, :, 0:LANES] = total.astype(BF16)
        target[o, :, LANES : 2 * LANES] = jnp.full((bins, LANES), mark_row.astype(F32)).astype(BF16)

    def spike_copy(o):
        return remote(
            spike_send.at[o], spike_recv.at[o], spike_ss.at[o], spike_rs.at[o], lax.rem(me + o, n)
        )

    def cot_copy(i):
        j = lax.rem(me + i, n)
        return remote(
            cot_hbm.at[pl.ds(j * sessions, sessions)],
            cot_recv.at[me],
            cot_ss.at[i],
            cot_rs.at[i],
            j,
        )

    def part_copy(o):
        return remote(
            part_send.at[o], part_recv.at[o], part_ss.at[o], part_rs.at[o], lax.rem(me - o + n, n)
        )

    def enc_copy(i):
        j = lax.rem(me + i, n)
        return remote(
            enc_send.at[j], encoded_hbm.at[mine], enc_ss.at[i], enc_rs.at[i], j
        )

    def grad_copy(o):
        return remote(
            grad_send.at[o], rows_hbm.at[o], grad_ss.at[o], grad_rs.at[o], lax.rem(me + o, n)
        )

    def start_all(copy):
        def step(i, carry):
            copy(i).start()
            return carry

        return step

    def wait_all(copy):
        def step(i, carry):
            copy(i).wait()
            return carry

        return step

    pl.semaphore_wait(barrier, n - 1)
    lax.fori_loop(1, NEAR, start_all(spike_copy), 0)
    lax.fori_loop(1, n, start_all(cot_copy), 0)

    q = lax.broadcasted_iota(jnp.int32, (encode_rows, bins), 0)
    c = lax.broadcasted_iota(jnp.int32, (encode_rows, bins), 1)
    same_bin = q // chunk * depth + lax.rem(q, depth) == c
    session = lax.rem(q, chunk) // depth
    for o in range(NEAR):
        route[o] = jnp.where(
            same_bin, jnp.where(session == owners[o], 1.0, 0.0), 0.0
        ).astype(BF16)

    loads[0].wait()
    lax.fori_loop(1, NEAR, wait_all(spike_copy), 0)

    per_tile = TILE // bins

    def project(step, carry):
        o = NEAR - per_tile - step * per_tile
        moved = spike_recv[pl.ds(o, per_tile)].reshape(TILE, 2 * LANES)
        values = moved[:, 0:LANES].astype(F32)
        holder = moved[:, LANES : 2 * LANES].astype(F32)
        spread = jnp.concatenate(
            [jnp.where(holder == float(k), values, 0.0).astype(BF16) for k in range(table_rows)],
            axis=1,
        )
        part_send[pl.ds(o, per_tile)] = (
            jnp.dot(spread, table[...], preferred_element_type=F32)
            .astype(BF16)
            .reshape(per_tile, bins, width)
        )

        def send(x, inner):
            @pl.when(o + x != 0)
            def _():
                part_copy(o + x).start()

            return inner

        lax.fori_loop(0, per_tile, send, 0)
        return carry

    lax.fori_loop(0, NEAR // per_tile, project, 0)
    part_recv[0] = part_send[0]
    for o in range(NEAR):
        marked_ref[:, o * bins : (o + 1) * bins] = (
            spike_recv[o].astype(F32).T.astype(BF16)
        )
    lax.fori_loop(1, NEAR, wait_all(part_copy), 0)
    loads[1].wait()
    loads[2].wait()

    hidden_tiles = w_in.shape[1] // FF_TILE
    chunks = TILE // chunk
    for e in range(encode_rows // TILE):
        here = pl.ds(e * TILE, TILE)
        total = jnp.zeros((TILE, width), F32)
        for o in range(NEAR):
            total = total + jnp.dot(
                route[o, here, :], part_recv[o], preferred_element_type=F32
            )
        inputs = total.astype(BF16).astype(F32)
        gain = gain_ref[...]
        inverse = lax.rsqrt(jnp.mean(inputs * inputs, axis=-1, keepdims=True) + EPS)
        normed = (inputs * inverse * gain).astype(BF16)
        accumulator[...] = inputs

        def forward(f, inner):
            cols = pl.ds(pl.multiple_of(f * FF_TILE, FF_TILE), FF_TILE)
            v = jnp.dot(normed, w_in[:, cols], preferred_element_type=F32)
            v2 = v * v
            th = jnp.tanh(GELU_C * (v + GELU_A * v * v2))
            half = 0.5 * (1.0 + th)
            slopes[:, cols] = half + 0.5 * v * (1.0 - th * th) * (
                GELU_C * (1.0 + 3.0 * GELU_A * v2)
            )
            accumulator[...] += jnp.dot(
                (v * half).astype(BF16), w_out[cols, :], preferred_element_type=F32
            )
            return inner

        lax.fori_loop(0, hidden_tiles, forward, 0)
        enc_send[e * chunks : (e + 1) * chunks] = (
            accumulator[...].reshape(chunks, sessions, depth, width).astype(BF16)
        )

        def send_encoded(x, inner):
            j = e * chunks + x

            @pl.when(j != me)
            def _():
                enc_copy(lax.rem(j - me + n, n)).start()

            return inner

        lax.fori_loop(0, chunks, send_encoded, 0)
        if e == 0:
            loads[3].wait()
            lax.fori_loop(1, n, wait_all(cot_copy), 0)
        cot = (
            cot_recv[e * chunks : (e + 1) * chunks].astype(F32).reshape(TILE, width).astype(BF16)
        )
        accumulator[...] = jnp.zeros_like(accumulator)

        def backward(f, inner):
            cols = pl.ds(pl.multiple_of(f * FF_TILE, FF_TILE), FF_TILE)
            back = lax.dot_general(
                cot, w_out[cols, :], (((1,), (1,)), ((), ())), preferred_element_type=F32
            )
            accumulator[...] += lax.dot_general(
                (back * slopes[:, cols]).astype(BF16),
                w_in[:, cols],
                (((1,), (1,)), ((), ())),
                preferred_element_type=F32,
            )
            return inner

        lax.fori_loop(0, hidden_tiles, backward, 0)
        scaled = accumulator[...] * gain
        grad = inverse * scaled - inputs * (inverse * inverse * inverse) * jnp.mean(
            scaled * inputs, axis=-1, keepdims=True
        )
        returned[here, :] = (cot.astype(F32) + grad).astype(BF16)

    def give_back(step, carry):
        o = NEAR - 1 - step
        grad_send[o] = lax.dot_general(
            route[o], returned[...], (((0,), (0,)), ((), ())), preferred_element_type=F32
        ).astype(BF16)

        @pl.when(o != 0)
        def _():
            grad_copy(o).start()

        return carry

    lax.fori_loop(0, NEAR, give_back, 0)
    keep = pltpu.make_async_copy(grad_send.at[0], rows_hbm.at[0], load_sems.at[4])
    keep.start()
    keep_encoded = pltpu.make_async_copy(enc_send.at[me], encoded_hbm.at[mine], load_sems.at[5])
    keep_encoded.start()
    keep.wait()
    keep_encoded.wait()
    lax.fori_loop(1, n, wait_all(enc_copy), 0)
    lax.fori_loop(1, NEAR, wait_all(grad_copy), 0)


def grad_kernel(per_step, marked_ref, rows_ref, out_ref):
    first = pl.program_id(0) * per_step
    values = marked_ref[0:LANES, :].astype(F32)
    holder = marked_ref[LANES : 2 * LANES, :].astype(F32)
    spread = jnp.concatenate(
        [
            jnp.where(holder == (first + k).astype(F32), values, 0.0).astype(BF16)
            for k in range(per_step)
        ],
        axis=0,
    )
    out_ref[...] = jnp.dot(spread, rows_ref[...], preferred_element_type=F32).astype(BF16)


def on_device(n, spikes, block_lists, bin_counts, readin_table, norm_gain, w_in, w_out, cotangent):
    sessions, bins, columns = spikes.shape
    table_rows, unit_block, width = readin_table.shape
    total_sessions, depth, _ = cotangent.shape
    hidden = w_in.shape[1]
    rows = NEAR * bins
    encode_rows = sessions * bins
    vmem = pl.BlockSpec(memory_space=pltpu.VMEM)
    smem = pl.BlockSpec(memory_space=pltpu.SMEM)
    hbm = pl.BlockSpec(memory_space=pl.ANY)
    near = pltpu.SemaphoreType.DMA((NEAR,))
    every = pltpu.SemaphoreType.DMA((n,))
    encoded, marked, grad_rows = pl.pallas_call(
        functools.partial(exchange_kernel, n, table_rows),
        out_shape=(
            jax.ShapeDtypeStruct((total_sessions, depth, width), BF16),
            jax.ShapeDtypeStruct((2 * LANES, rows), BF16),
            jax.ShapeDtypeStruct((NEAR, bins, width), BF16),
        ),
        in_specs=[smem, smem, vmem, hbm, vmem, hbm, hbm, hbm],
        out_specs=(hbm, vmem, hbm),
        scratch_shapes=[
            pltpu.VMEM((table_rows * unit_block, width), BF16),
            pltpu.VMEM((width, hidden), BF16),
            pltpu.VMEM((hidden, width), BF16),
            pltpu.VMEM((NEAR, bins, 2 * LANES), BF16),
            pltpu.VMEM((NEAR, bins, 2 * LANES), BF16),
            pltpu.VMEM((NEAR, bins, width), BF16),
            pltpu.VMEM((NEAR, bins, width), BF16),
            pltpu.VMEM((n, sessions, depth, width), BF16),
            pltpu.VMEM((n, sessions, depth, width), BF16),
            pltpu.VMEM((NEAR, encode_rows, bins), BF16),
            pltpu.VMEM((encode_rows, width), BF16),
            pltpu.VMEM((NEAR, bins, width), BF16),
            pltpu.VMEM((TILE, hidden), F32),
            pltpu.VMEM((TILE, width), F32),
            pltpu.SemaphoreType.DMA((6,)),
            near,
            near,
            near,
            near,
            near,
            near,
            every,
            every,
            every,
            every,
        ],
        compiler_params=pltpu.CompilerParams(
            collective_id=0, has_side_effects=True, vmem_limit_bytes=58 * 1024 * 1024
        ),
    )(
        block_lists,
        bin_counts,
        spikes,
        readin_table.reshape(table_rows * unit_block, width),
        norm_gain.reshape(1, width),
        w_in,
        w_out,
        cotangent,
    )
    per_step = 4
    total = pl.pallas_call(
        functools.partial(grad_kernel, per_step),
        grid=(table_rows // per_step,),
        out_shape=jax.ShapeDtypeStruct((table_rows * unit_block, width), BF16),
        in_specs=[
            pl.BlockSpec((2 * LANES, rows), lambda i: (0, 0)),
            pl.BlockSpec((rows, width), lambda i: (0, 0)),
        ],
        out_specs=pl.BlockSpec((per_step * unit_block, width), lambda i: (i, 0)),
        compiler_params=pltpu.CompilerParams(vmem_limit_bytes=40 * 1024 * 1024),
    )(marked, grad_rows.reshape(rows, width))
    return (encoded, total.reshape(table_rows, unit_block, width))


def solution(mesh):
    n = mesh.shape["dp"]
    return jax.shard_map(
        functools.partial(on_device, n),
        mesh=mesh,
        in_specs=(
            P("dp", None, None),
            P("dp", None),
            P("dp"),
            P("dp", None, None),
            P(),
            P(),
            P(),
            P(None, "dp", None),
        ),
        out_specs=(P(None, "dp", None), P("dp", None, None)),
        check_vma=False,
    )
```

```python
import functools

import jax
import jax.numpy as jnp
from jax import lax
from jax.experimental import pallas as pl
from jax.experimental.pallas import tpu as pltpu
from jax.sharding import PartitionSpec as P

NEAR = 8
SHIFT = NEAR // 2
EPS = 1e-06
LANES = 128
TILE = 256
FF_TILE = 512
GELU_C = 0.7978845608028654
GELU_A = 0.044715
BF16 = jnp.bfloat16
F32 = jnp.float32


def remote(src, dst, send_sem, recv_sem, device):
    return pltpu.make_async_remote_copy(
        src_ref=src,
        dst_ref=dst,
        send_sem=send_sem,
        recv_sem=recv_sem,
        device_id=(device,),
        device_id_type=pl.DeviceIdType.MESH,
    )


def exchange_kernel(
    n,
    table_rows,
    lists_ref,
    counts_ref,
    spikes_ref,
    table_hbm,
    gain_ref,
    w_in_hbm,
    w_out_hbm,
    cot_hbm,
    encoded_hbm,
    marked_ref,
    rows_hbm,
    table,
    w_in,
    w_out,
    spike_send,
    spike_recv,
    part_send,
    part_recv,
    cot_recv,
    enc_send,
    route,
    returned,
    grad_send,
    slopes,
    accumulator,
    load_sems,
    spike_ss,
    spike_rs,
    part_ss,
    part_rs,
    grad_ss,
    grad_rs,
    cot_ss,
    cot_rs,
    enc_ss,
    enc_rs,
):
    me = lax.axis_index("dp")
    sessions, bins, _ = spikes_ref.shape
    blocks = 2
    depth = bins // n
    chunk = sessions * depth
    width = table.shape[1]
    rows = NEAR * bins
    encode_rows = returned.shape[0]
    mine = pl.ds(lax.rem(me - SHIFT + n, n) * sessions, sessions)
    loads = [
        pltpu.make_async_copy(table_hbm, table, load_sems.at[0]),
        pltpu.make_async_copy(w_in_hbm, w_in, load_sems.at[1]),
        pltpu.make_async_copy(w_out_hbm, w_out, load_sems.at[2]),
        pltpu.make_async_copy(cot_hbm.at[mine], cot_recv.at[me], load_sems.at[3]),
    ]
    for load in loads:
        load.start()

    barrier = pltpu.get_barrier_semaphore()

    def greet(i, carry):
        pl.semaphore_signal(
            barrier,
            inc=1,
            device_id=(lax.rem(me + i, n),),
            device_id_type=pl.DeviceIdType.MESH,
        )
        return carry

    lax.fori_loop(1, n, greet, 0)

    offsets = []
    locals_ = []
    for i in range(sessions * blocks):
        entry = lists_ref[i // blocks, i % blocks]
        offsets.append(lax.rem(entry // table_rows - me + n, n))
        locals_.append(lax.rem(entry, table_rows))
    valid = [
        lax.broadcasted_iota(jnp.int32, (bins, LANES), 0) < counts_ref[s] for s in range(sessions)
    ]
    slabs = []
    for s in range(sessions):
        for b in range(blocks):
            slab = spikes_ref[s, :, b * LANES : (b + 1) * LANES].astype(F32)
            slabs.append(jnp.where(valid[s], slab, 0.0))
    lane = lax.broadcasted_iota(jnp.int32, (bins, LANES), 1)
    marks = jnp.zeros((bins, LANES), F32)
    for i in range(sessions * blocks):
        marks = marks + jnp.where(lane == offsets[i] + 1, float(i // blocks), 0.0)
    for o in range(NEAR):
        total = jnp.zeros((bins, LANES), F32)
        mark_row = jnp.int32(0)
        for i in range(sessions * blocks):
            hit = jnp.where(offsets[i] == o, 1, 0)
            total = total + slabs[i] * hit.astype(F32)
            mark_row = mark_row + hit * locals_[i]
        target = spike_recv if o == 0 else spike_send
        target[o, :, 0:LANES] = total.astype(BF16)
        target[o, :, LANES : 2 * LANES] = jnp.where(
            lane == 0, mark_row.astype(F32), marks
        ).astype(BF16)

    def spike_copy(o):
        return remote(
            spike_send.at[o], spike_recv.at[o], spike_ss.at[o], spike_rs.at[o], lax.rem(me + o, n)
        )

    def cot_copy(i):
        j = lax.rem(me + i, n)
        return remote(
            cot_hbm.at[pl.ds(lax.rem(j - SHIFT + n, n) * sessions, sessions)],
            cot_recv.at[me],
            cot_ss.at[i],
            cot_rs.at[i],
            j,
        )

    def part_copy(o):
        return remote(
            part_send.at[o], part_recv.at[o], part_ss.at[o], part_rs.at[o], lax.rem(me - o + SHIFT + n, n)
        )

    def enc_copy(i):
        j = lax.rem(me + i, n)
        return remote(
            enc_send.at[j], encoded_hbm.at[mine], enc_ss.at[i], enc_rs.at[i], j
        )

    def grad_copy(o):
        return remote(
            grad_send.at[o],
            rows_hbm.at[o],
            grad_ss.at[o],
            grad_rs.at[o],
            lax.rem(me - SHIFT + o + n, n),
        )

    def start_all(copy):
        def step(i, carry):
            copy(i).start()
            return carry

        return step

    def wait_all(copy):
        def step(i, carry):
            copy(i).wait()
            return carry

        return step

    pl.semaphore_wait(barrier, n - 1)
    lax.fori_loop(1, NEAR, start_all(spike_copy), 0)
    lax.fori_loop(1, n, start_all(cot_copy), 0)

    loads[0].wait()
    lax.fori_loop(1, NEAR, wait_all(spike_copy), 0)

    per_tile = TILE // bins
    others = [o for o in range(NEAR) if o != SHIFT]

    def project(step, carry):
        o = NEAR - per_tile - step * per_tile
        moved = spike_recv[pl.ds(o, per_tile)].reshape(TILE, 2 * LANES)
        values = moved[:, 0:LANES].astype(F32)
        holder = moved[:, LANES : 2 * LANES].astype(F32)[:, 0:1]
        spread = jnp.concatenate(
            [jnp.where(holder == float(k), values, 0.0).astype(BF16) for k in range(table_rows)],
            axis=1,
        )
        part_send[pl.ds(o, per_tile)] = (
            jnp.dot(spread, table[...], preferred_element_type=F32)
            .astype(BF16)
            .reshape(per_tile, bins, width)
        )

        def send(x, inner):
            @pl.when(o + x != SHIFT)
            def _():
                part_copy(o + x).start()

            return inner

        lax.fori_loop(0, per_tile, send, 0)
        return carry

    lax.fori_loop(0, NEAR // per_tile, project, 0)
    part_recv[SHIFT] = part_send[SHIFT]

    q = lax.broadcasted_iota(jnp.int32, (encode_rows, bins), 0)
    c = lax.broadcasted_iota(jnp.int32, (encode_rows, bins), 1)
    same_bin = q // chunk * depth + lax.rem(q, depth) == c
    session = (lax.rem(q, chunk) // depth).astype(F32)
    marks = spike_recv[SHIFT, 0:16, LANES : 2 * LANES].astype(F32)
    for o in range(NEAR):
        route[o] = jnp.where(
            same_bin, jnp.where(session == marks[0:1, 1 + o : 2 + o], 1.0, 0.0), 0.0
        ).astype(BF16)

    for o in range(NEAR):
        marked_ref[:, o * bins : (o + 1) * bins] = (
            spike_recv[o].astype(F32).T.astype(BF16)
        )
    for o in others:
        part_copy(o).wait()
    loads[1].wait()
    loads[2].wait()

    hidden_tiles = w_in.shape[1] // FF_TILE
    chunks = TILE // chunk
    for e in range(encode_rows // TILE):
        here = pl.ds(e * TILE, TILE)
        total = jnp.zeros((TILE, width), F32)
        for o in range(NEAR):
            total = total + jnp.dot(
                route[o, here, :], part_recv[o], preferred_element_type=F32
            )
        inputs = total.astype(BF16).astype(F32)
        gain = gain_ref[...]
        inverse = lax.rsqrt(jnp.mean(inputs * inputs, axis=-1, keepdims=True) + EPS)
        normed = (inputs * inverse * gain).astype(BF16)
        accumulator[...] = inputs

        def forward(f, inner):
            cols = pl.ds(pl.multiple_of(f * FF_TILE, FF_TILE), FF_TILE)
            v = jnp.dot(normed, w_in[:, cols], preferred_element_type=F32)
            v2 = v * v
            th = jnp.tanh(GELU_C * (v + GELU_A * v * v2))
            half = 0.5 * (1.0 + th)
            slopes[:, cols] = half + 0.5 * v * (1.0 - th * th) * (
                GELU_C * (1.0 + 3.0 * GELU_A * v2)
            )
            accumulator[...] += jnp.dot(
                (v * half).astype(BF16), w_out[cols, :], preferred_element_type=F32
            )
            return inner

        lax.fori_loop(0, hidden_tiles, forward, 0)
        enc_send[e * chunks : (e + 1) * chunks] = (
            accumulator[...].reshape(chunks, sessions, depth, width).astype(BF16)
        )

        def send_encoded(x, inner):
            j = e * chunks + x

            @pl.when(j != me)
            def _():
                enc_copy(lax.rem(j - me + n, n)).start()

            return inner

        lax.fori_loop(0, chunks, send_encoded, 0)
        if e == 0:
            loads[3].wait()
            lax.fori_loop(1, n, wait_all(cot_copy), 0)
        cot = (
            cot_recv[e * chunks : (e + 1) * chunks].astype(F32).reshape(TILE, width).astype(BF16)
        )
        accumulator[...] = jnp.zeros_like(accumulator)

        def backward(f, inner):
            cols = pl.ds(pl.multiple_of(f * FF_TILE, FF_TILE), FF_TILE)
            back = lax.dot_general(
                cot, w_out[cols, :], (((1,), (1,)), ((), ())), preferred_element_type=F32
            )
            accumulator[...] += lax.dot_general(
                (back * slopes[:, cols]).astype(BF16),
                w_in[:, cols],
                (((1,), (1,)), ((), ())),
                preferred_element_type=F32,
            )
            return inner

        lax.fori_loop(0, hidden_tiles, backward, 0)
        scaled = accumulator[...] * gain
        grad = inverse * scaled - inputs * (inverse * inverse * inverse) * jnp.mean(
            scaled * inputs, axis=-1, keepdims=True
        )
        returned[here, :] = (cot.astype(F32) + grad).astype(BF16)

    def give_back(step, carry):
        o = NEAR - 1 - step
        grad_send[o] = lax.dot_general(
            route[o], returned[...], (((0,), (0,)), ((), ())), preferred_element_type=F32
        ).astype(BF16)

        @pl.when(o != SHIFT)
        def _():
            grad_copy(o).start()

        return carry

    lax.fori_loop(0, NEAR, give_back, 0)
    keep = pltpu.make_async_copy(grad_send.at[SHIFT], rows_hbm.at[SHIFT], load_sems.at[4])
    keep.start()
    keep_encoded = pltpu.make_async_copy(enc_send.at[me], encoded_hbm.at[mine], load_sems.at[5])
    keep_encoded.start()
    keep.wait()
    keep_encoded.wait()
    lax.fori_loop(1, n, wait_all(enc_copy), 0)
    for o in others:
        grad_copy(o).wait()


def grad_kernel(per_step, marked_ref, rows_ref, out_ref):
    first = pl.program_id(0) * per_step
    values = marked_ref[0:LANES, :].astype(F32)
    holder = marked_ref[LANES : 2 * LANES, :].astype(F32)[0:1, :]
    spread = jnp.concatenate(
        [
            jnp.where(holder == (first + k).astype(F32), values, 0.0).astype(BF16)
            for k in range(per_step)
        ],
        axis=0,
    )
    out_ref[...] = jnp.dot(spread, rows_ref[...], preferred_element_type=F32).astype(BF16)


def on_device(n, spikes, block_lists, bin_counts, readin_table, norm_gain, w_in, w_out, cotangent):
    sessions, bins, columns = spikes.shape
    table_rows, unit_block, width = readin_table.shape
    total_sessions, depth, _ = cotangent.shape
    hidden = w_in.shape[1]
    rows = NEAR * bins
    encode_rows = sessions * bins
    vmem = pl.BlockSpec(memory_space=pltpu.VMEM)
    smem = pl.BlockSpec(memory_space=pltpu.SMEM)
    hbm = pl.BlockSpec(memory_space=pl.ANY)
    near = pltpu.SemaphoreType.DMA((NEAR,))
    every = pltpu.SemaphoreType.DMA((n,))
    encoded, marked, grad_rows = pl.pallas_call(
        functools.partial(exchange_kernel, n, table_rows),
        out_shape=(
            jax.ShapeDtypeStruct((total_sessions, depth, width), BF16),
            jax.ShapeDtypeStruct((2 * LANES, rows), BF16),
            jax.ShapeDtypeStruct((NEAR, bins, width), BF16),
        ),
        in_specs=[smem, smem, vmem, hbm, vmem, hbm, hbm, hbm],
        out_specs=(hbm, vmem, hbm),
        scratch_shapes=[
            pltpu.VMEM((table_rows * unit_block, width), BF16),
            pltpu.VMEM((width, hidden), BF16),
            pltpu.VMEM((hidden, width), BF16),
            pltpu.VMEM((NEAR, bins, 2 * LANES), BF16),
            pltpu.VMEM((NEAR, bins, 2 * LANES), BF16),
            pltpu.VMEM((NEAR, bins, width), BF16),
            pltpu.VMEM((NEAR, bins, width), BF16),
            pltpu.VMEM((n, sessions, depth, width), BF16),
            pltpu.VMEM((n, sessions, depth, width), BF16),
            pltpu.VMEM((NEAR, encode_rows, bins), BF16),
            pltpu.VMEM((encode_rows, width), BF16),
            pltpu.VMEM((NEAR, bins, width), BF16),
            pltpu.VMEM((TILE, hidden), F32),
            pltpu.VMEM((TILE, width), F32),
            pltpu.SemaphoreType.DMA((6,)),
            near,
            near,
            near,
            near,
            near,
            near,
            every,
            every,
            every,
            every,
        ],
        compiler_params=pltpu.CompilerParams(
            collective_id=0, has_side_effects=True, vmem_limit_bytes=58 * 1024 * 1024
        ),
    )(
        block_lists,
        bin_counts,
        spikes,
        readin_table.reshape(table_rows * unit_block, width),
        norm_gain.reshape(1, width),
        w_in,
        w_out,
        cotangent,
    )
    per_step = 4
    total = pl.pallas_call(
        functools.partial(grad_kernel, per_step),
        grid=(table_rows // per_step,),
        out_shape=jax.ShapeDtypeStruct((table_rows * unit_block, width), BF16),
        in_specs=[
            pl.BlockSpec((2 * LANES, rows), lambda i: (0, 0)),
            pl.BlockSpec((rows, width), lambda i: (0, 0)),
        ],
        out_specs=pl.BlockSpec((per_step * unit_block, width), lambda i: (i, 0)),
        compiler_params=pltpu.CompilerParams(vmem_limit_bytes=40 * 1024 * 1024),
    )(marked, grad_rows.reshape(rows, width))
    return (encoded, total.reshape(table_rows, unit_block, width))


def solution(mesh):
    n = mesh.shape["dp"]
    return jax.shard_map(
        functools.partial(on_device, n),
        mesh=mesh,
        in_specs=(
            P("dp", None, None),
            P("dp", None),
            P("dp"),
            P("dp", None, None),
            P(),
            P(),
            P(),
            P(None, "dp", None),
        ),
        out_specs=(P(None, "dp", None), P("dp", None, None)),
        check_vma=False,
    )
```

```python
import functools

import jax
import jax.numpy as jnp
from jax import lax
from jax.experimental import pallas as pl
from jax.experimental.pallas import tpu as pltpu
from jax.sharding import PartitionSpec as P

NEAR = 8
SHIFT = NEAR // 2
EPS = 1e-06
LANES = 128
TILE = 256
FF_TILE = 1024
GELU_C = 0.7978845608028654
GELU_A = 0.044715
BF16 = jnp.bfloat16
F32 = jnp.float32


def remote(src, dst, send_sem, recv_sem, device):
    return pltpu.make_async_remote_copy(
        src_ref=src,
        dst_ref=dst,
        send_sem=send_sem,
        recv_sem=recv_sem,
        device_id=(device,),
        device_id_type=pl.DeviceIdType.MESH,
    )


def exchange_kernel(
    n,
    table_rows,
    lists_ref,
    counts_ref,
    spikes_ref,
    table_hbm,
    gain_ref,
    w_in_hbm,
    w_out_hbm,
    cot_hbm,
    encoded_hbm,
    marked_ref,
    rows_hbm,
    table,
    w_in,
    w_out,
    spike_send,
    spike_recv,
    part_send,
    part_recv,
    cot_recv,
    enc_send,
    route,
    returned,
    grad_send,
    slopes,
    accumulator,
    load_sems,
    spike_ss,
    spike_rs,
    part_ss,
    part_rs,
    grad_ss,
    grad_rs,
    cot_ss,
    cot_rs,
    enc_ss,
    enc_rs,
):
    me = lax.axis_index("dp")
    sessions, bins, _ = spikes_ref.shape
    blocks = 2
    depth = bins // n
    chunk = sessions * depth
    width = table.shape[1]
    rows = NEAR * bins
    encode_rows = returned.shape[0]
    mine = pl.ds(lax.rem(me - SHIFT + n, n) * sessions, sessions)
    loads = [
        pltpu.make_async_copy(table_hbm, table, load_sems.at[0]),
        pltpu.make_async_copy(w_in_hbm, w_in, load_sems.at[1]),
        pltpu.make_async_copy(w_out_hbm, w_out, load_sems.at[2]),
        pltpu.make_async_copy(cot_hbm.at[mine], cot_recv.at[me], load_sems.at[3]),
    ]
    for load in loads:
        load.start()

    barrier = pltpu.get_barrier_semaphore()

    def greet(i, carry):
        pl.semaphore_signal(
            barrier,
            inc=1,
            device_id=(lax.rem(me + i, n),),
            device_id_type=pl.DeviceIdType.MESH,
        )
        return carry

    lax.fori_loop(1, n, greet, 0)

    offsets = []
    locals_ = []
    for i in range(sessions * blocks):
        entry = lists_ref[i // blocks, i % blocks]
        offsets.append(lax.rem(entry // table_rows - me + n, n))
        locals_.append(lax.rem(entry, table_rows))
    valid = [
        lax.broadcasted_iota(jnp.int32, (bins, LANES), 0) < counts_ref[s] for s in range(sessions)
    ]
    slabs = []
    for s in range(sessions):
        for b in range(blocks):
            slab = spikes_ref[s, :, b * LANES : (b + 1) * LANES].astype(F32)
            slabs.append(jnp.where(valid[s], slab, 0.0))
    lane = lax.broadcasted_iota(jnp.int32, (bins, LANES), 1)
    marks = jnp.zeros((bins, LANES), F32)
    for i in range(sessions * blocks):
        marks = marks + jnp.where(lane == offsets[i] + 1, float(i // blocks), 0.0)
    for o in range(NEAR):
        total = jnp.zeros((bins, LANES), F32)
        mark_row = jnp.int32(0)
        for i in range(sessions * blocks):
            hit = jnp.where(offsets[i] == o, 1, 0)
            total = total + slabs[i] * hit.astype(F32)
            mark_row = mark_row + hit * locals_[i]
        target = spike_recv if o == 0 else spike_send
        target[o, :, 0:LANES] = total.astype(BF16)
        target[o, :, LANES : 2 * LANES] = jnp.where(
            lane == 0, mark_row.astype(F32), marks
        ).astype(BF16)

    def spike_copy(o):
        return remote(
            spike_send.at[o], spike_recv.at[o], spike_ss.at[o], spike_rs.at[o], lax.rem(me + o, n)
        )

    def cot_copy(i):
        j = lax.rem(me + i, n)
        return remote(
            cot_hbm.at[pl.ds(lax.rem(j - SHIFT + n, n) * sessions, sessions)],
            cot_recv.at[me],
            cot_ss.at[i],
            cot_rs.at[i],
            j,
        )

    def part_copy(o):
        return remote(
            part_send.at[o], part_recv.at[o], part_ss.at[o], part_rs.at[o], lax.rem(me - o + SHIFT + n, n)
        )

    def enc_copy(i):
        j = lax.rem(me + i, n)
        return remote(
            enc_send.at[j], encoded_hbm.at[mine], enc_ss.at[i], enc_rs.at[i], j
        )

    def grad_copy(o):
        return remote(
            grad_send.at[o],
            rows_hbm.at[o],
            grad_ss.at[o],
            grad_rs.at[o],
            lax.rem(me - SHIFT + o + n, n),
        )

    def start_all(copy):
        def step(i, carry):
            copy(i).start()
            return carry

        return step

    def wait_all(copy):
        def step(i, carry):
            copy(i).wait()
            return carry

        return step

    pl.semaphore_wait(barrier, n - 1)
    lax.fori_loop(1, NEAR, start_all(spike_copy), 0)
    lax.fori_loop(1, n, start_all(cot_copy), 0)

    loads[0].wait()
    lax.fori_loop(1, NEAR, wait_all(spike_copy), 0)

    per_tile = TILE // bins
    others = [o for o in range(NEAR) if o != SHIFT]

    def project(step, carry):
        o = NEAR - per_tile - step * per_tile
        moved = spike_recv[pl.ds(o, per_tile)].reshape(TILE, 2 * LANES)
        values = moved[:, 0:LANES].astype(F32)
        holder = moved[:, LANES : 2 * LANES].astype(F32)[:, 0:1]
        spread = jnp.concatenate(
            [jnp.where(holder == float(k), values, 0.0).astype(BF16) for k in range(table_rows)],
            axis=1,
        )
        part_send[pl.ds(o, per_tile)] = (
            jnp.dot(spread, table[...], preferred_element_type=F32)
            .astype(BF16)
            .reshape(per_tile, bins, width)
        )

        def send(x, inner):
            @pl.when(o + x != SHIFT)
            def _():
                part_copy(o + x).start()

            return inner

        lax.fori_loop(0, per_tile, send, 0)
        return carry

    lax.fori_loop(0, NEAR // per_tile, project, 0)
    part_recv[SHIFT] = part_send[SHIFT]

    q = lax.broadcasted_iota(jnp.int32, (bins, encode_rows), 1)
    c = lax.broadcasted_iota(jnp.int32, (bins, encode_rows), 0)
    same_bin = q // chunk * depth + lax.rem(q, depth) == c
    session = (lax.rem(q, chunk) // depth).astype(F32)
    marks = spike_recv[SHIFT, 0:16, LANES : 2 * LANES].astype(F32)
    for o in range(NEAR):
        route[o] = jnp.where(
            same_bin, jnp.where(session == marks[0:1, 1 + o : 2 + o], 1.0, 0.0), 0.0
        ).astype(BF16)

    for o in range(NEAR):
        marked_ref[:, o * bins : (o + 1) * bins] = (
            spike_recv[o].astype(F32).T.astype(BF16)
        )
    for o in others:
        part_copy(o).wait()
    loads[1].wait()
    loads[2].wait()

    hidden_tiles = w_in.shape[1] // FF_TILE
    chunks = TILE // chunk
    for e in range(encode_rows // TILE):
        here = pl.ds(e * TILE, TILE)
        total = lax.dot_general(
            route[:, :, here].reshape(rows, TILE),
            part_recv[...].reshape(rows, width),
            (((0,), (0,)), ((), ())),
            preferred_element_type=F32,
        )
        inputs = total.astype(BF16).astype(F32)
        gain = gain_ref[...]
        inverse = lax.rsqrt(jnp.mean(inputs * inputs, axis=-1, keepdims=True) + EPS)
        normed = (inputs * inverse * gain).astype(BF16)
        accumulator[...] = inputs

        def forward(f, inner):
            cols = pl.ds(pl.multiple_of(f * FF_TILE, FF_TILE), FF_TILE)
            v = jnp.dot(normed, w_in[:, cols], preferred_element_type=F32)
            v2 = v * v
            th = jnp.tanh(GELU_C * (v + GELU_A * v * v2))
            half = 0.5 * (1.0 + th)
            slopes[:, cols] = half + 0.5 * v * (1.0 - th * th) * (
                GELU_C * (1.0 + 3.0 * GELU_A * v2)
            )
            accumulator[...] += jnp.dot(
                (v * half).astype(BF16), w_out[cols, :], preferred_element_type=F32
            )
            return inner

        lax.fori_loop(0, hidden_tiles, forward, 0)
        enc_send[e * chunks : (e + 1) * chunks] = (
            accumulator[...].reshape(chunks, sessions, depth, width).astype(BF16)
        )

        def send_encoded(x, inner):
            j = e * chunks + x

            @pl.when(j != me)
            def _():
                enc_copy(lax.rem(j - me + n, n)).start()

            return inner

        lax.fori_loop(0, chunks, send_encoded, 0)
        if e == 0:
            loads[3].wait()
            lax.fori_loop(1, n, wait_all(cot_copy), 0)
        cot = (
            cot_recv[e * chunks : (e + 1) * chunks].astype(F32).reshape(TILE, width).astype(BF16)
        )
        accumulator[...] = jnp.zeros_like(accumulator)

        def backward(f, inner):
            cols = pl.ds(pl.multiple_of(f * FF_TILE, FF_TILE), FF_TILE)
            back = lax.dot_general(
                cot, w_out[cols, :], (((1,), (1,)), ((), ())), preferred_element_type=F32
            )
            accumulator[...] += lax.dot_general(
                (back * slopes[:, cols]).astype(BF16),
                w_in[:, cols],
                (((1,), (1,)), ((), ())),
                preferred_element_type=F32,
            )
            return inner

        lax.fori_loop(0, hidden_tiles, backward, 0)
        scaled = accumulator[...] * gain
        grad = inverse * scaled - inputs * (inverse * inverse * inverse) * jnp.mean(
            scaled * inputs, axis=-1, keepdims=True
        )
        returned[here, :] = (cot.astype(F32) + grad).astype(BF16)

    def give_back(step, carry):
        o = NEAR - per_tile - step * per_tile
        grad_send[pl.ds(o, per_tile)] = (
            jnp.dot(
                route[pl.ds(o, per_tile)].reshape(TILE, encode_rows),
                returned[...],
                preferred_element_type=F32,
            )
            .astype(BF16)
            .reshape(per_tile, bins, width)
        )

        def send(x, inner):
            @pl.when(o + x != SHIFT)
            def _():
                grad_copy(o + x).start()

            return inner

        lax.fori_loop(0, per_tile, send, 0)
        return carry

    lax.fori_loop(0, NEAR // per_tile, give_back, 0)
    keep = pltpu.make_async_copy(grad_send.at[SHIFT], rows_hbm.at[SHIFT], load_sems.at[4])
    keep.start()
    keep_encoded = pltpu.make_async_copy(enc_send.at[me], encoded_hbm.at[mine], load_sems.at[5])
    keep_encoded.start()
    keep.wait()
    keep_encoded.wait()
    lax.fori_loop(1, n, wait_all(enc_copy), 0)
    for o in others:
        grad_copy(o).wait()


def grad_kernel(per_step, marked_ref, rows_ref, out_ref):
    first = pl.program_id(0) * per_step
    values = marked_ref[0:LANES, :].astype(F32)
    holder = marked_ref[LANES : 2 * LANES, :].astype(F32)[0:1, :]
    spread = jnp.concatenate(
        [
            jnp.where(holder == (first + k).astype(F32), values, 0.0).astype(BF16)
            for k in range(per_step)
        ],
        axis=0,
    )
    out_ref[...] = jnp.dot(spread, rows_ref[...], preferred_element_type=F32).astype(BF16)


def on_device(n, spikes, block_lists, bin_counts, readin_table, norm_gain, w_in, w_out, cotangent):
    sessions, bins, columns = spikes.shape
    table_rows, unit_block, width = readin_table.shape
    total_sessions, depth, _ = cotangent.shape
    hidden = w_in.shape[1]
    rows = NEAR * bins
    encode_rows = sessions * bins
    vmem = pl.BlockSpec(memory_space=pltpu.VMEM)
    smem = pl.BlockSpec(memory_space=pltpu.SMEM)
    hbm = pl.BlockSpec(memory_space=pl.ANY)
    near = pltpu.SemaphoreType.DMA((NEAR,))
    every = pltpu.SemaphoreType.DMA((n,))
    encoded, marked, grad_rows = pl.pallas_call(
        functools.partial(exchange_kernel, n, table_rows),
        out_shape=(
            jax.ShapeDtypeStruct((total_sessions, depth, width), BF16),
            jax.ShapeDtypeStruct((2 * LANES, rows), BF16),
            jax.ShapeDtypeStruct((NEAR, bins, width), BF16),
        ),
        in_specs=[smem, smem, vmem, hbm, vmem, hbm, hbm, hbm],
        out_specs=(hbm, vmem, hbm),
        scratch_shapes=[
            pltpu.VMEM((table_rows * unit_block, width), BF16),
            pltpu.VMEM((width, hidden), BF16),
            pltpu.VMEM((hidden, width), BF16),
            pltpu.VMEM((NEAR, bins, 2 * LANES), BF16),
            pltpu.VMEM((NEAR, bins, 2 * LANES), BF16),
            pltpu.VMEM((NEAR, bins, width), BF16),
            pltpu.VMEM((NEAR, bins, width), BF16),
            pltpu.VMEM((n, sessions, depth, width), BF16),
            pltpu.VMEM((n, sessions, depth, width), BF16),
            pltpu.VMEM((NEAR, bins, encode_rows), BF16),
            pltpu.VMEM((encode_rows, width), BF16),
            pltpu.VMEM((NEAR, bins, width), BF16),
            pltpu.VMEM((TILE, hidden), F32),
            pltpu.VMEM((TILE, width), F32),
            pltpu.SemaphoreType.DMA((6,)),
            near,
            near,
            near,
            near,
            near,
            near,
            every,
            every,
            every,
            every,
        ],
        compiler_params=pltpu.CompilerParams(
            collective_id=0, has_side_effects=True, vmem_limit_bytes=58 * 1024 * 1024
        ),
    )(
        block_lists,
        bin_counts,
        spikes,
        readin_table.reshape(table_rows * unit_block, width),
        norm_gain.reshape(1, width),
        w_in,
        w_out,
        cotangent,
    )
    per_step = 4
    total = pl.pallas_call(
        functools.partial(grad_kernel, per_step),
        grid=(table_rows // per_step,),
        out_shape=jax.ShapeDtypeStruct((table_rows * unit_block, width), BF16),
        in_specs=[
            pl.BlockSpec((2 * LANES, rows), lambda i: (0, 0)),
            pl.BlockSpec((rows, width), lambda i: (0, 0)),
        ],
        out_specs=pl.BlockSpec((per_step * unit_block, width), lambda i: (i, 0)),
        compiler_params=pltpu.CompilerParams(vmem_limit_bytes=58 * 1024 * 1024),
    )(marked, grad_rows.reshape(rows, width))
    return (encoded, total.reshape(table_rows, unit_block, width))


def solution(mesh):
    n = mesh.shape["dp"]
    return jax.shard_map(
        functools.partial(on_device, n),
        mesh=mesh,
        in_specs=(
            P("dp", None, None),
            P("dp", None),
            P("dp"),
            P("dp", None, None),
            P(),
            P(),
            P(),
            P(None, "dp", None),
        ),
        out_specs=(P(None, "dp", None), P("dp", None, None)),
        check_vma=False,
    )
```

```python
import functools

import jax
import jax.numpy as jnp
from jax import lax
from jax.experimental import pallas as pl
from jax.experimental.pallas import tpu as pltpu
from jax.sharding import PartitionSpec as P

NEAR = 8
SHIFT = NEAR // 2
EPS = 1e-06
LANES = 128
TILE = 256
FF_TILE = 1024
GELU_C = 0.7978845608028654
GELU_A = 0.044715
BF16 = jnp.bfloat16
F32 = jnp.float32


def remote(src, dst, send_sem, recv_sem, device):
    return pltpu.make_async_remote_copy(
        src_ref=src,
        dst_ref=dst,
        send_sem=send_sem,
        recv_sem=recv_sem,
        device_id=(device,),
        device_id_type=pl.DeviceIdType.MESH,
    )


def exchange_kernel(
    n,
    table_rows,
    lists_ref,
    counts_ref,
    spikes_ref,
    table_hbm,
    gain_ref,
    w_in_hbm,
    w_out_hbm,
    cot_hbm,
    encoded_hbm,
    marked_ref,
    rows_hbm,
    table,
    w_in,
    w_out,
    spike_send,
    spike_recv,
    part_send,
    part_recv,
    cot_recv,
    enc_send,
    route,
    returned,
    grad_send,
    slopes,
    accumulator,
    load_sems,
    spike_ss,
    spike_rs,
    part_ss,
    part_rs,
    grad_ss,
    grad_rs,
    cot_ss,
    cot_rs,
    enc_ss,
    enc_rs,
):
    me = lax.axis_index("dp")
    sessions, bins, _ = spikes_ref.shape
    blocks = 2
    depth = bins // n
    chunk = sessions * depth
    width = table.shape[1]
    rows = NEAR * bins
    encode_rows = returned.shape[0]
    mine = pl.ds(lax.rem(me - SHIFT + n, n) * sessions, sessions)
    loads = [
        pltpu.make_async_copy(table_hbm, table, load_sems.at[0]),
        pltpu.make_async_copy(w_in_hbm, w_in, load_sems.at[1]),
        pltpu.make_async_copy(w_out_hbm, w_out, load_sems.at[2]),
        pltpu.make_async_copy(cot_hbm.at[mine], cot_recv.at[me], load_sems.at[3]),
    ]
    for load in loads:
        load.start()

    barrier = pltpu.get_barrier_semaphore()

    def greet(i, carry):
        pl.semaphore_signal(
            barrier,
            inc=1,
            device_id=(lax.rem(me + i, n),),
            device_id_type=pl.DeviceIdType.MESH,
        )
        return carry

    lax.fori_loop(1, n, greet, 0)

    offsets = []
    locals_ = []
    for i in range(sessions * blocks):
        entry = lists_ref[i // blocks, i % blocks]
        offsets.append(lax.rem(entry // table_rows - me + n, n))
        locals_.append(lax.rem(entry, table_rows))
    valid = [
        lax.broadcasted_iota(jnp.int32, (bins, LANES), 0) < counts_ref[s] for s in range(sessions)
    ]
    slabs = []
    for s in range(sessions):
        for b in range(blocks):
            slab = spikes_ref[s, :, b * LANES : (b + 1) * LANES].astype(F32)
            slabs.append(jnp.where(valid[s], slab, 0.0))
    lane = lax.broadcasted_iota(jnp.int32, (bins, LANES), 1)
    marks = jnp.zeros((bins, LANES), F32)
    for i in range(sessions * blocks):
        marks = marks + jnp.where(lane == offsets[i] + 1, float(i // blocks), 0.0)
    for o in range(NEAR):
        total = jnp.zeros((bins, LANES), F32)
        mark_row = jnp.int32(0)
        for i in range(sessions * blocks):
            hit = jnp.where(offsets[i] == o, 1, 0)
            total = total + slabs[i] * hit.astype(F32)
            mark_row = mark_row + hit * locals_[i]
        target = spike_recv if o == 0 else spike_send
        target[o, :, 0:LANES] = total.astype(BF16)
        target[o, :, LANES : 2 * LANES] = jnp.where(
            lane == 0, mark_row.astype(F32), marks
        ).astype(BF16)

    def spike_copy(o):
        return remote(
            spike_send.at[o], spike_recv.at[o], spike_ss.at[o], spike_rs.at[o], lax.rem(me + o, n)
        )

    def cot_copy(i):
        j = lax.rem(me + i, n)
        return remote(
            cot_hbm.at[pl.ds(lax.rem(j - SHIFT + n, n) * sessions, sessions)],
            cot_recv.at[me],
            cot_ss.at[i],
            cot_rs.at[i],
            j,
        )

    def part_copy(o):
        return remote(
            part_send.at[o], part_recv.at[o], part_ss.at[o], part_rs.at[o], lax.rem(me - o + SHIFT + n, n)
        )

    def enc_copy(i):
        j = lax.rem(me + i, n)
        return remote(
            enc_send.at[j], encoded_hbm.at[mine], enc_ss.at[i], enc_rs.at[i], j
        )

    def grad_copy(o):
        return remote(
            grad_send.at[o],
            rows_hbm.at[o],
            grad_ss.at[o],
            grad_rs.at[o],
            lax.rem(me - SHIFT + o + n, n),
        )

    def start_all(copy):
        def step(i, carry):
            copy(i).start()
            return carry

        return step

    def wait_all(copy):
        def step(i, carry):
            copy(i).wait()
            return carry

        return step

    pl.semaphore_wait(barrier, n - 1)
    lax.fori_loop(1, NEAR, start_all(spike_copy), 0)

    loads[0].wait()
    lax.fori_loop(1, NEAR, wait_all(spike_copy), 0)

    per_tile = TILE // bins
    others = [o for o in range(NEAR) if o != SHIFT]

    def project(step, carry):
        o = NEAR - per_tile - step * per_tile
        moved = spike_recv[pl.ds(o, per_tile)].reshape(TILE, 2 * LANES)
        values = moved[:, 0:LANES].astype(F32)
        holder = moved[:, LANES : 2 * LANES].astype(F32)[:, 0:1]
        spread = jnp.concatenate(
            [jnp.where(holder == float(k), values, 0.0).astype(BF16) for k in range(table_rows)],
            axis=1,
        )
        part_send[pl.ds(o, per_tile)] = (
            jnp.dot(spread, table[...], preferred_element_type=F32)
            .astype(BF16)
            .reshape(per_tile, bins, width)
        )

        def send(x, inner):
            @pl.when(o + x != SHIFT)
            def _():
                part_copy(o + x).start()

            return inner

        lax.fori_loop(0, per_tile, send, 0)
        return carry

    lax.fori_loop(0, NEAR // per_tile, project, 0)
    lax.fori_loop(1, n, start_all(cot_copy), 0)
    part_recv[SHIFT] = part_send[SHIFT]

    q = lax.broadcasted_iota(jnp.int32, (bins, encode_rows), 1)
    c = lax.broadcasted_iota(jnp.int32, (bins, encode_rows), 0)
    same_bin = q // chunk * depth + lax.rem(q, depth) == c
    session = (lax.rem(q, chunk) // depth).astype(F32)
    marks = spike_recv[SHIFT, 0:16, LANES : 2 * LANES].astype(F32)
    for o in range(NEAR):
        route[o] = jnp.where(
            same_bin, jnp.where(session == marks[0:1, 1 + o : 2 + o], 1.0, 0.0), 0.0
        ).astype(BF16)

    for o in range(NEAR):
        marked_ref[:, o * bins : (o + 1) * bins] = (
            spike_recv[o].astype(F32).T.astype(BF16)
        )
    for o in others:
        part_copy(o).wait()
    loads[1].wait()
    loads[2].wait()

    hidden_tiles = w_in.shape[1] // FF_TILE
    chunks = TILE // chunk
    for e in range(encode_rows // TILE):
        here = pl.ds(e * TILE, TILE)
        total = lax.dot_general(
            route[:, :, here].reshape(rows, TILE),
            part_recv[...].reshape(rows, width),
            (((0,), (0,)), ((), ())),
            preferred_element_type=F32,
        )
        inputs = total.astype(BF16).astype(F32)
        gain = gain_ref[...]
        inverse = lax.rsqrt(jnp.mean(inputs * inputs, axis=-1, keepdims=True) + EPS)
        normed = (inputs * inverse * gain).astype(BF16)
        accumulator[...] = inputs

        def forward(f, inner):
            cols = pl.ds(pl.multiple_of(f * FF_TILE, FF_TILE), FF_TILE)
            v = jnp.dot(normed, w_in[:, cols], preferred_element_type=F32)
            v2 = v * v
            th = jnp.tanh(GELU_C * (v + GELU_A * v * v2))
            half = 0.5 * (1.0 + th)
            slopes[:, cols] = half + 0.5 * v * (1.0 - th * th) * (
                GELU_C * (1.0 + 3.0 * GELU_A * v2)
            )
            accumulator[...] += jnp.dot(
                (v * half).astype(BF16), w_out[cols, :], preferred_element_type=F32
            )
            return inner

        lax.fori_loop(0, hidden_tiles, forward, 0)
        enc_send[e * chunks : (e + 1) * chunks] = (
            accumulator[...].reshape(chunks, sessions, depth, width).astype(BF16)
        )

        def send_encoded(x, inner):
            j = e * chunks + x

            @pl.when(j != me)
            def _():
                enc_copy(lax.rem(j - me + n, n)).start()

            return inner

        lax.fori_loop(0, chunks, send_encoded, 0)
        if e == 0:
            loads[3].wait()
            lax.fori_loop(1, n, wait_all(cot_copy), 0)
        cot = (
            cot_recv[e * chunks : (e + 1) * chunks].astype(F32).reshape(TILE, width).astype(BF16)
        )
        accumulator[...] = jnp.zeros_like(accumulator)

        def backward(f, inner):
            cols = pl.ds(pl.multiple_of(f * FF_TILE, FF_TILE), FF_TILE)
            back = lax.dot_general(
                cot, w_out[cols, :], (((1,), (1,)), ((), ())), preferred_element_type=F32
            )
            accumulator[...] += lax.dot_general(
                (back * slopes[:, cols]).astype(BF16),
                w_in[:, cols],
                (((1,), (1,)), ((), ())),
                preferred_element_type=F32,
            )
            return inner

        lax.fori_loop(0, hidden_tiles, backward, 0)
        scaled = accumulator[...] * gain
        grad = inverse * scaled - inputs * (inverse * inverse * inverse) * jnp.mean(
            scaled * inputs, axis=-1, keepdims=True
        )
        returned[here, :] = (cot.astype(F32) + grad).astype(BF16)

    def give_back(step, carry):
        o = NEAR - per_tile - step * per_tile
        grad_send[pl.ds(o, per_tile)] = (
            jnp.dot(
                route[pl.ds(o, per_tile)].reshape(TILE, encode_rows),
                returned[...],
                preferred_element_type=F32,
            )
            .astype(BF16)
            .reshape(per_tile, bins, width)
        )

        def send(x, inner):
            @pl.when(o + x != SHIFT)
            def _():
                grad_copy(o + x).start()

            return inner

        lax.fori_loop(0, per_tile, send, 0)
        return carry

    lax.fori_loop(0, NEAR // per_tile, give_back, 0)
    keep = pltpu.make_async_copy(grad_send.at[SHIFT], rows_hbm.at[SHIFT], load_sems.at[4])
    keep.start()
    keep_encoded = pltpu.make_async_copy(enc_send.at[me], encoded_hbm.at[mine], load_sems.at[5])
    keep_encoded.start()
    keep.wait()
    keep_encoded.wait()
    lax.fori_loop(1, n, wait_all(enc_copy), 0)
    for o in others:
        grad_copy(o).wait()


def grad_kernel(per_step, marked_ref, rows_ref, out_ref):
    first = pl.program_id(0) * per_step
    values = marked_ref[0:LANES, :].astype(F32)
    holder = marked_ref[LANES : 2 * LANES, :].astype(F32)[0:1, :]
    spread = jnp.concatenate(
        [
            jnp.where(holder == (first + k).astype(F32), values, 0.0).astype(BF16)
            for k in range(per_step)
        ],
        axis=0,
    )
    out_ref[...] = jnp.dot(spread, rows_ref[...], preferred_element_type=F32).astype(BF16)


def on_device(n, spikes, block_lists, bin_counts, readin_table, norm_gain, w_in, w_out, cotangent):
    sessions, bins, columns = spikes.shape
    table_rows, unit_block, width = readin_table.shape
    total_sessions, depth, _ = cotangent.shape
    hidden = w_in.shape[1]
    rows = NEAR * bins
    encode_rows = sessions * bins
    vmem = pl.BlockSpec(memory_space=pltpu.VMEM)
    smem = pl.BlockSpec(memory_space=pltpu.SMEM)
    hbm = pl.BlockSpec(memory_space=pl.ANY)
    near = pltpu.SemaphoreType.DMA((NEAR,))
    every = pltpu.SemaphoreType.DMA((n,))
    encoded, marked, grad_rows = pl.pallas_call(
        functools.partial(exchange_kernel, n, table_rows),
        out_shape=(
            jax.ShapeDtypeStruct((total_sessions, depth, width), BF16),
            jax.ShapeDtypeStruct((2 * LANES, rows), BF16),
            jax.ShapeDtypeStruct((NEAR, bins, width), BF16),
        ),
        in_specs=[smem, smem, vmem, hbm, vmem, hbm, hbm, hbm],
        out_specs=(hbm, vmem, hbm),
        scratch_shapes=[
            pltpu.VMEM((table_rows * unit_block, width), BF16),
            pltpu.VMEM((width, hidden), BF16),
            pltpu.VMEM((hidden, width), BF16),
            pltpu.VMEM((NEAR, bins, 2 * LANES), BF16),
            pltpu.VMEM((NEAR, bins, 2 * LANES), BF16),
            pltpu.VMEM((NEAR, bins, width), BF16),
            pltpu.VMEM((NEAR, bins, width), BF16),
            pltpu.VMEM((n, sessions, depth, width), BF16),
            pltpu.VMEM((n, sessions, depth, width), BF16),
            pltpu.VMEM((NEAR, bins, encode_rows), BF16),
            pltpu.VMEM((encode_rows, width), BF16),
            pltpu.VMEM((NEAR, bins, width), BF16),
            pltpu.VMEM((TILE, hidden), F32),
            pltpu.VMEM((TILE, width), F32),
            pltpu.SemaphoreType.DMA((6,)),
            near,
            near,
            near,
            near,
            near,
            near,
            every,
            every,
            every,
            every,
        ],
        compiler_params=pltpu.CompilerParams(
            collective_id=0, has_side_effects=True, vmem_limit_bytes=58 * 1024 * 1024
        ),
    )(
        block_lists,
        bin_counts,
        spikes,
        readin_table.reshape(table_rows * unit_block, width),
        norm_gain.reshape(1, width),
        w_in,
        w_out,
        cotangent,
    )
    per_step = 4
    total = pl.pallas_call(
        functools.partial(grad_kernel, per_step),
        grid=(table_rows // per_step,),
        out_shape=jax.ShapeDtypeStruct((table_rows * unit_block, width), BF16),
        in_specs=[
            pl.BlockSpec((2 * LANES, rows), lambda i: (0, 0)),
            pl.BlockSpec((rows, width), lambda i: (0, 0)),
        ],
        out_specs=pl.BlockSpec((per_step * unit_block, width), lambda i: (i, 0)),
        compiler_params=pltpu.CompilerParams(vmem_limit_bytes=58 * 1024 * 1024),
    )(marked, grad_rows.reshape(rows, width))
    return (encoded, total.reshape(table_rows, unit_block, width))


def solution(mesh):
    n = mesh.shape["dp"]
    return jax.shard_map(
        functools.partial(on_device, n),
        mesh=mesh,
        in_specs=(
            P("dp", None, None),
            P("dp", None),
            P("dp"),
            P("dp", None, None),
            P(),
            P(),
            P(),
            P(None, "dp", None),
        ),
        out_specs=(P(None, "dp", None), P("dp", None, None)),
        check_vma=False,
    )
```
